32 devices in a mesh: grp: 2 (over x), lon: 16 (over z, y, core).
Axes of the slice: x: 2, y: 2, z: 4, core: 2. Of those that a mesh axis runs over, the one named last changes fastest.
Arguments:
- fields: bfloat16 [1024, 16, 1440], P(('grp', 'lon')), parts along dimension 0, may hold values from -6 to 6
- filter_basis: bfloat16 [16, 3, 6, 32, 96], P('lon'), may hold values from -0.4375 to 0.4375
- offsets: int32 [16, 6], P('lon'), may hold values from 0 to 44, as said below
- counts: int32 [16], P('lon'), may hold values from 1 to 6
- mixing: bfloat16 [512, 1536], replicated, may hold values from -0.15625 to 0.15625
- cotangent: bfloat16 [1024, 16, 1440], P('grp', 'lon'), parts along dimension 0, may hold values from -6 to 6
Outputs:
- mixed_out: bfloat16 [1024, 16, 1440], P('grp', 'lon'), parts along dimension 0
- field_grad: bfloat16 [1024, 16, 1440], P(('grp', 'lon')), parts along dimension 0
- mixing_grad: float32 [1024, 1536], P(('grp', 'lon')), parts along dimension 0
The draws below stay inside these ranges and needn't reach their ends.
There are 2 independent parts, one for each index of `grp`. The reference program is written for one: setup_inputs(seed, part) draws one part's arguments, and reference() takes and returns one part's arrays. A program takes and returns all parts, laid end to end along the dimension named above; an argument that names none is the same for every part. Nothing has to cross between parts.
Inputs may be any that keep to these rules, and one draw needn't show every extreme that they name: The 6 block offsets of a row are distinct.
All inputs are finite; a program needn't handle non-finite values.
Results may differ from the reference program's by a relative error of at most 0.006.
Values may be sent and summed in bfloat16 or wider, within the bound.
A program may use at most 128 MiB of HBM per device.

```python
import jax
import jax.numpy as jnp
from jax import lax

C = 512
LON = 1440
K = 3
LB = 32
NNZ = 6
NB = 45
LAT = 16


def draw_offsets(key, part):
    key = jax.random.fold_in(key, 11)
    moves = jax.random.randint(key, (LAT,), -3, 4)
    moves = moves.at[0].set(0)
    steps = jnp.arange(NNZ, dtype=jnp.int32)
    centred = (steps + 1) // 2 * jnp.where(steps % 2 == 1, 1, -1)
    return ((moves[:, None] + centred[None, :]) % NB).astype(jnp.int32)


def draw_counts(key, part):
    key = jax.random.fold_in(key, 23)
    places = jnp.arange(LAT, dtype=jnp.int32)
    edge = jnp.minimum(places, LAT - 1 - places)
    base = jnp.maximum(1, NNZ - edge * 4 * NNZ // LAT)
    extra = jax.random.randint(key, (LAT,), 0, 2)
    extra = extra.at[LAT // 2].set(0)
    return jnp.minimum(NNZ, base + extra).astype(jnp.int32)


def strengthened(entries, own_key, source, target, parts, factor):
    owner, partner = [(jnp.arange(entries.shape[position]) // (entries.shape[position] // parts)).reshape([-1 if axis == position else 1 for axis in range(entries.ndim)]) for position in (source, target)]
    chosen = jax.random.permutation(own_key, parts)[partner]
    strong = (owner == chosen) | (owner == (partner + parts // 2) % parts)
    return jnp.where(strong, factor * entries, entries)


def block_levels(key, dims, split, least, high):
    loudness = 1.0
    for position, blocks in split:
        steps = jax.random.uniform(jax.random.fold_in(jax.random.fold_in(key, 6), position), (blocks,), jnp.float32, least / len(split), high / len(split))
        loudness = loudness * jnp.repeat(jnp.exp(steps), dims[position] // blocks).reshape((-1,) + (1,) * (len(dims) - 1 - position))
    return loudness


def bell_draw(own_key, shape, width, reach, pieces=(), kind=jnp.bfloat16):
    array = jax.random.normal(own_key, shape, jnp.float32) * width
    if len(pieces) > 0:
        array = block_levels(own_key, shape, pieces, -0.22, 0.18) * array
    return jnp.clip(array, min=-reach, max=reach).astype(kind)


def bell_draw_with(stream_key, shape, scale, most, split, heavy, kind=jnp.bfloat16):
    entries = scale * jax.random.normal(stream_key, shape, jnp.float32)
    if split:
        entries = entries * block_levels(stream_key, shape, split, -0.22, 0.18)
    return jnp.clip(strengthened(entries, jax.random.fold_in(stream_key, 3), *heavy), -most, most).astype(kind)


def setup_inputs(seed: int = 0, part: int = 0) -> dict:
    splits = jax.random.split(jax.random.key(seed), 7)
    part_splits = jax.random.split(jax.random.fold_in(splits[6], part), 7)
    fields = bell_draw(part_splits[0], (C, LAT, LON), 1.0, 6.0, ((0, 16),))
    filter_basis = bell_draw(splits[1], (LAT, 3, NNZ, LB, K * LB), (6 * LB) ** -0.5, 0.4375, ((0, 16),))
    offsets = draw_offsets(jax.random.fold_in(splits[6], 71), part)
    counts = draw_counts(jax.random.fold_in(splits[6], 71), part)
    mixing = bell_draw(splits[4], (C, C * K), (K * C) ** -0.5, 0.15625)
    cotangent = bell_draw_with(part_splits[5], (C, LAT, LON), 1.0, 6.0, ((1, 16),), (1, 0, 16, 2.0))
    return {"fields": fields, "filter_basis": filter_basis, "offsets": offsets, "counts": counts, "mixing": mixing, "cotangent": cotangent}


def contract_rows(extended, filter_basis, offsets, counts):
    channels = extended.shape[0]
    rows = filter_basis.shape[0]

    def one_row(row_index):
        window = lax.dynamic_slice_in_dim(extended, row_index, 3, 1).reshape(channels, 3, NB, LB)
        doubled = jnp.concatenate([window, window], 2)
        weights = filter_basis[row_index].astype(jnp.float32)
        offset_row = offsets[row_index]

        def add_slot(slot, total):
            shifted = lax.dynamic_slice_in_dim(doubled, offset_row[slot], NB, 2)
            piece = lax.dynamic_index_in_dim(weights, slot, 1, keepdims=False)
            return total + jnp.einsum('cdbi,dij->cbj', shifted, piece)

        total = lax.fori_loop(0, counts[row_index], add_slot, jnp.zeros((channels, NB, K * LB), jnp.float32))
        return total.reshape(channels, NB, K, LB).transpose(0, 2, 1, 3).reshape(channels, K, LON)

    mapped = lax.map(one_row, jnp.arange(rows, dtype=jnp.int32))
    return mapped.transpose(1, 2, 0, 3)


def adjoint_rows(grads, filter_basis, offsets, counts):
    channels = grads.shape[0]
    rows = filter_basis.shape[0]

    def one_row(row_index):
        row = lax.dynamic_index_in_dim(grads, row_index, 2, keepdims=False)
        row = row.reshape(channels, K, NB, LB).transpose(0, 2, 1, 3).reshape(channels, NB, K * LB)
        weights = filter_basis[row_index].astype(jnp.float32)
        offset_row = offsets[row_index]

        def add_slot(slot, total):
            piece = lax.dynamic_index_in_dim(weights, slot, 1, keepdims=False)
            term = jnp.einsum('cbj,dij->cdbi', row, piece)
            doubled = jnp.concatenate([term, term], 2)
            start = (NB - offset_row[slot]) % NB
            return total + lax.dynamic_slice_in_dim(doubled, start, NB, 2)

        total = lax.fori_loop(0, counts[row_index], add_slot, jnp.zeros((channels, 3, NB, LB), jnp.float32))
        return total.reshape(channels, 3, LON)

    mapped = lax.map(one_row, jnp.arange(rows, dtype=jnp.int32))
    spread = jnp.zeros((channels, rows + 2, LON), jnp.float32)
    for shift_rows in range(3):
        spread = spread + jnp.pad(mapped[:, :, shift_rows].transpose(1, 0, 2), ((0, 0), (shift_rows, 2 - shift_rows), (0, 0)))
    return spread


def reference(fields, filter_basis, offsets, counts, mixing, cotangent):
    field_wide = fields.astype(jnp.float32)
    extended = jnp.pad(field_wide, ((0, 0), (1, 1), (0, 0)))
    features = contract_rows(extended, filter_basis, offsets, counts).astype(jnp.bfloat16)
    flat = features.astype(jnp.float32).reshape(C * K, LAT, LON)
    mixing_wide = mixing.astype(jnp.float32)
    mixed = jnp.einsum('om,mrp->orp', mixing_wide, flat)
    mixed_out = (field_wide + mixed).astype(jnp.bfloat16)
    cot_wide = cotangent.astype(jnp.float32)
    feature_grad = jnp.einsum('om,orp->mrp', mixing_wide, cot_wide).astype(jnp.bfloat16)
    mixing_grad = jnp.einsum('orp,mrp->om', cot_wide, flat)
    spread = adjoint_rows(feature_grad.astype(jnp.float32).reshape(C, K, LAT, LON), filter_basis, offsets, counts)
    field_grad = (cot_wide + spread[:, 1:-1]).astype(jnp.bfloat16)
    return mixed_out, field_grad, mixing_grad
```

```python
import functools

import jax
import jax.numpy as jnp
from jax import lax
from jax.experimental import pallas as pl
from jax.experimental.pallas import tpu as pltpu
from jax.sharding import PartitionSpec as P

F32 = jnp.float32
BF16 = jnp.bfloat16


def spread_columns(channels, kernels, dtype):
    size = channels * kernels
    row = lax.broadcasted_iota(jnp.int32, (size, size), 0)
    col = lax.broadcasted_iota(jnp.int32, (size, size), 1)
    return ((row % channels) * kernels + row // channels == col).astype(dtype)


def adjoint_kernel(kernels, block, slots, off_ref, cot_ref, mix_ref, w_ref, a0_ref, a1_ref, a2_ref, g_ref):
    width, channels = cot_ref.shape
    nblocks = width // block
    rows = block * 9

    @pl.loop(0, width // rows)
    def _(step):
        at = pl.ds(pl.multiple_of(step * rows, rows), rows)
        for k in range(kernels):
            g_ref[at, k * channels:(k + 1) * channels] = jnp.dot(
                cot_ref[at, :], mix_ref[:, k * channels:(k + 1) * channels], preferred_element_type=F32
            ).astype(BF16)

    @pl.loop(0, nblocks)
    def _(b):
        parts = []
        for s in range(slots):
            src = b - off_ref[0, s]
            src = jnp.where(src < 0, src + nblocks, src)
            at = pl.ds(pl.multiple_of(src * block, block), block)
            for k in range(kernels):
                parts.append(g_ref[at, k * channels:(k + 1) * channels])
        out = jnp.dot(w_ref[...], jnp.concatenate(parts, axis=0), preferred_element_type=F32)
        at = pl.ds(pl.multiple_of(b * block, block), block)
        a0_ref[at, :] = out[:block].astype(BF16)
        a1_ref[at, :] = out[block:2 * block] + cot_ref[at, :].astype(F32)
        a2_ref[at, :] = out[2 * block:].astype(BF16)


def forward_kernel(kernels, block, slots, off_ref, x0_ref, x1_ref, x2_ref, cot_ref, mix_ref, w_ref,
                   out_ref, grad_ref, f_ref):
    width, channels = x1_ref.shape
    nblocks = width // block
    rows = block * 9

    @pl.loop(0, nblocks)
    def _(b):
        parts = []
        for s in range(slots):
            src = b + off_ref[0, s]
            src = jnp.where(src >= nblocks, src - nblocks, src)
            at = pl.ds(pl.multiple_of(src * block, block), block)
            for x_ref in (x0_ref, x1_ref, x2_ref):
                parts.append(x_ref[at, :])
        out = jnp.dot(w_ref[...], jnp.concatenate(parts, axis=0), preferred_element_type=F32).astype(BF16)
        at = pl.ds(pl.multiple_of(b * block, block), block)
        for k in range(kernels):
            f_ref[at, k * channels:(k + 1) * channels] = out[k * block:(k + 1) * block]

    @pl.loop(0, width // rows)
    def _(step):
        at = pl.ds(pl.multiple_of(step * rows, rows), rows)
        mixed = lax.dot_general(
            f_ref[at, :], mix_ref[...], (((1,), (1,)), ((), ())), preferred_element_type=F32
        )
        out_ref[at, :] = (x1_ref[at, :].astype(F32) + mixed).astype(BF16)

    for k in range(kernels):
        grad_ref[:, k * channels:(k + 1) * channels] = jnp.dot(
            cot_ref[...], f_ref[:, k * channels:(k + 1) * channels], preferred_element_type=F32
        ).astype(grad_ref.dtype)


def passed_along(value, axis, steps):
    count = lax.axis_size(axis)
    leading, last = (max(0, -steps), min(count, count - steps))
    return lax.ppermute(value, axis, [(source, source + steps) for source in range(leading, last)])


def local(fields, filter_basis, offsets, counts, mixing, cotangent):
    channels, cols = mixing.shape
    kernels = cols // channels
    _, taps, slots, block, outer = filter_basis.shape
    width = fields.shape[2]
    vmem = pl.BlockSpec(memory_space=pltpu.VMEM)
    smem = pl.BlockSpec(memory_space=pltpu.SMEM)
    params = pltpu.CompilerParams(vmem_limit_bytes=48 * 2**20)

    own = lax.all_to_all(fields.transpose(1, 0, 2), "lon", split_axis=0, concat_axis=0, tiled=True)
    own = own.reshape(channels, width)

    live = jnp.arange(slots) < counts[0]
    basis = jnp.where(live[None, :, None, None], filter_basis[0], 0)
    w_adj = basis.transpose(0, 2, 1, 3).reshape(taps * block, slots * outer)
    w_fwd = basis.transpose(3, 1, 0, 2).reshape(outer, slots * taps * block)
    perm = spread_columns(channels, kernels, BF16)
    mix = lax.dot_general(mixing, perm, (((1,), (1,)), ((), ())), preferred_element_type=F32).astype(BF16)
    cot = cotangent[:, 0, :]
    cot_t = cot.T

    a0, a1, a2 = pl.pallas_call(
        functools.partial(adjoint_kernel, kernels, block, slots),
        out_shape=[
            jax.ShapeDtypeStruct((width, channels), BF16),
            jax.ShapeDtypeStruct((width, channels), F32),
            jax.ShapeDtypeStruct((width, channels), BF16),
        ],
        in_specs=[smem, vmem, vmem, vmem],
        out_specs=[vmem] * 3,
        scratch_shapes=[pltpu.VMEM((width, cols), BF16)],
        compiler_params=params,
        cost_estimate=pl.CostEstimate(flops=3 * 10**10, bytes_accessed=10**7, transcendentals=0),
        name="adjoint",
    )(offsets, cot_t, mix, w_adj)
    from_next = passed_along(a0, "lon", -1)
    from_prev = passed_along(a2, "lon", 1)

    own_t = own.T
    below = passed_along(own_t, "lon", 1)
    above = passed_along(own_t, "lon", -1)

    banded = (a1 + from_next.astype(F32) + from_prev.astype(F32)).astype(BF16).T
    banded = banded.reshape(lax.axis_size("lon"), -1, width)
    field_grad = lax.all_to_all(banded, "lon", split_axis=0, concat_axis=0, tiled=True).transpose(1, 0, 2)

    mixed_t, grad = pl.pallas_call(
        functools.partial(forward_kernel, kernels, block, slots),
        out_shape=[
            jax.ShapeDtypeStruct((width, channels), BF16),
            jax.ShapeDtypeStruct((channels, cols), F32),
        ],
        in_specs=[smem] + [vmem] * 6,
        out_specs=[vmem] * 2,
        scratch_shapes=[pltpu.VMEM((width, cols), BF16)],
        compiler_params=params,
        cost_estimate=pl.CostEstimate(flops=3 * 10**10, bytes_accessed=10**7, transcendentals=0),
        name="forward",
    )(offsets, below, own_t, above, cot, mix, w_fwd)
    grad = lax.psum_scatter(grad, "lon", scatter_dimension=0, tiled=True)
    grad = lax.dot(grad, spread_columns(channels, kernels, F32), precision=lax.Precision.HIGHEST)
    return mixed_t.T[:, None, :], field_grad, grad


def solution(mesh):
    in_specs = (
        P(("grp", "lon"), None, None),
        P("lon", None, None, None, None),
        P("lon", None),
        P("lon"),
        P(),
        P("grp", "lon", None),
    )
    out_specs = (P("grp", "lon", None), P(("grp", "lon"), None, None), P(("grp", "lon"), None))
    return jax.shard_map(local, mesh=mesh, in_specs=in_specs, out_specs=out_specs, check_vma=False)
```

```python
import functools

import jax
import jax.numpy as jnp
from jax import lax
from jax.experimental import pallas as pl
from jax.experimental.pallas import tpu as pltpu
from jax.sharding import PartitionSpec as P

F32 = jnp.float32
BF16 = jnp.bfloat16


def spread_columns(channels, kernels, dtype):
    size = channels * kernels
    row = lax.broadcasted_iota(jnp.int32, (size, size), 0)
    col = lax.broadcasted_iota(jnp.int32, (size, size), 1)
    return ((row % channels) * kernels + row // channels == col).astype(dtype)


def fused_kernel(kernels, block, slots, sections, to_ref, from_ref, fields_ref, cot_t_ref, cot_ref, mix_ref, wa_ref, wf_ref,
                 mixed_ref, fg_ref, grad_ref,
                 rows_ref, x_ref, gf_ref, a0_ref, a1_ref, a2_ref, h0_ref, h2_ref, band_ref,
                 part_ref, pair_ref, sum_ref, got_ref,
                 f_send, f_recv, x_send, x_recv, h_send, h_recv, b_send, b_recv, p_send, p_recv, g_send, g_recv):
    width, channels = cot_t_ref.shape
    nblocks = width // block
    n, per_device, _ = fields_ref.shape
    tile = 128
    groups = channels // tile
    per_group = tile // per_device
    me = lax.axis_index("lon")
    core = lax.rem(me, 2)
    pair = me + 1 - 2 * core
    cols = lambda k: slice(k * channels, (k + 1) * channels)
    has_prev, has_next = me > 0, me < n - 1

    def remote(src, dst, send, recv, device):
        return pltpu.make_async_remote_copy(
            src_ref=src, dst_ref=dst, send_sem=send, recv_sem=recv,
            device_id={"lon": device}, device_id_type=pl.DeviceIdType.MESH)

    def peer_of(i):
        return lax.rem(me + i, n)

    barrier = pltpu.get_barrier_semaphore()

    @pl.loop(1, n)
    def _(i):
        pl.semaphore_signal(barrier, inc=1, device_id={"lon": peer_of(i)}, device_id_type=pl.DeviceIdType.MESH)
    pl.semaphore_wait(barrier, n - 1)

    def field_copy(i):
        peer = peer_of(i)
        return remote(fields_ref.at[peer], rows_ref.at[me], f_send.at[i], f_recv.at[me], peer)

    @pl.loop(1, n)
    def _(i):
        field_copy(i).start()
    rows_ref[me] = fields_ref[me]

    @pl.when(jnp.logical_not(has_prev))
    def _():
        x_ref[0] = jnp.zeros((nblocks, block, channels), BF16)
        h2_ref[...] = jnp.zeros((width, channels), BF16)

    @pl.when(jnp.logical_not(has_next))
    def _():
        x_ref[2] = jnp.zeros((nblocks, block, channels), BF16)
        h0_ref[...] = jnp.zeros((width, channels), BF16)

    some = nblocks // 5
    rows = some * block

    @pl.loop(0, 5)
    def _(step):
        at = pl.ds(pl.multiple_of(step * rows, rows), rows)
        for k in range(kernels):
            gf_ref[pl.ds(step * some, some), :, cols(k)] = jnp.dot(
                cot_t_ref[at, :], mix_ref[:, cols(k)], preferred_element_type=F32
            ).astype(BF16).reshape(some, block, channels)

    piece = width // sections

    def down_copy(t):
        at = slice(t * piece, (t + 1) * piece)
        return remote(a0_ref.at[at], h0_ref.at[at], h_send.at[0, t], h_recv.at[0, t], me - 1)

    def up_copy(t):
        at = slice(t * piece, (t + 1) * piece)
        return remote(a2_ref.at[at], h2_ref.at[at], h_send.at[1, t], h_recv.at[1, t], me + 1)

    for t in range(sections):
        @pl.loop(t * (nblocks // sections), (t + 1) * (nblocks // sections))
        def _(b):
            parts = []
            for s in range(slots):
                found = gf_ref[from_ref[s, b]]
                for k in range(kernels):
                    parts.append(found[:, cols(k)])
            out = jnp.dot(wa_ref[...], jnp.concatenate(parts, axis=0), preferred_element_type=F32)
            at = pl.ds(pl.multiple_of(b * block, block), block)
            a0_ref[at, :] = out[:block].astype(BF16)
            a1_ref[at, :] = out[block:2 * block] + cot_t_ref[at, :].astype(F32)
            a2_ref[at, :] = out[2 * block:].astype(BF16)

        @pl.when(has_prev)
        def _():
            down_copy(t).start()

        @pl.when(has_next)
        def _():
            up_copy(t).start()

    def row_copy(to_next, g):
        at = (slice(None), slice(None), slice(g * tile, (g + 1) * tile))
        which, device = (0, me + 1) if to_next else (2, me - 1)
        return remote(x_ref.at[(1,) + at], x_ref.at[(which,) + at],
                      x_send.at[which // 2, g], x_recv.at[which // 2, g], device)

    for g in range(groups):
        @pl.loop(g * per_group, (g + 1) * per_group)
        def _(j):
            @pl.when(j != me)
            def _():
                remote(fields_ref.at[j], rows_ref.at[j], f_send.at[0], f_recv.at[j], pair).wait_recv()
        for start in range(0, width, tile):
            stop = min(start + tile, width)
            x_ref[1, start // block:stop // block, :, g * tile:(g + 1) * tile] = rows_ref[
                g * per_group:(g + 1) * per_group, :, start:stop
            ].reshape(tile, stop - start).T.reshape((stop - start) // block, block, tile)

        @pl.when(has_next)
        def _():
            row_copy(True, g).start()

        @pl.when(has_prev)
        def _():
            row_copy(False, g).start()

    for t in range(sections):
        @pl.when(has_next)
        def _():
            down_copy(t).wait_recv()

        @pl.when(has_prev)
        def _():
            up_copy(t).wait_recv()
    for start in range(0, width, tile):
        stop = min(start + tile, width)
        total = (a1_ref[start:stop] + h0_ref[start:stop].astype(F32) + h2_ref[start:stop].astype(F32)).astype(BF16)
        band_ref[:, :, start:stop] = total.T.reshape(n, per_device, stop - start)

    def band_copy(i):
        peer = peer_of(i)
        return remote(band_ref.at[peer], fg_ref.at[me], b_send.at[i], b_recv.at[me], peer)

    @pl.loop(1, n)
    def _(i):
        band_copy(i).start()
    fg_ref[me] = band_ref[me]

    for g in range(groups):
        @pl.when(has_prev)
        def _():
            row_copy(True, g).wait_recv()

        @pl.when(has_next)
        def _():
            row_copy(False, g).wait_recv()

    @pl.loop(0, nblocks)
    def _(b):
        parts = []
        for s in range(slots):
            for d in range(3):
                parts.append(x_ref[d, to_ref[s, b]])
        out = jnp.dot(wf_ref[...], jnp.concatenate(parts, axis=0), preferred_element_type=F32).astype(BF16)
        for k in range(kernels):
            gf_ref[b, :, cols(k)] = out[k * block:(k + 1) * block]

    half = channels // 2

    def pair_copy(k):
        return remote(part_ref.at[k, 1 - core], pair_ref.at[k], p_send.at[k], p_recv.at[k], pair)

    for k in range(kernels):
        part_ref[k] = jnp.dot(
            cot_ref[...], gf_ref[:, :, cols(k)].reshape(width, channels), preferred_element_type=F32
        ).reshape(2, half, channels)
        pair_copy(k).start()

    @pl.loop(0, 5)
    def _(step):
        at = pl.ds(pl.multiple_of(step * rows, rows), rows)
        blocks = pl.ds(step * some, some)
        mixed = lax.dot_general(
            gf_ref[blocks].reshape(rows, kernels * channels), mix_ref[...],
            (((1,), (1,)), ((), ())), preferred_element_type=F32)
        mixed_ref[at, :] = (x_ref[1, blocks].reshape(rows, channels).astype(F32) + mixed).astype(BF16)

    chips = n // 2
    chip = me // 2
    for k in range(kernels):
        pair_copy(k).wait_recv()
        sum_ref[:, :, cols(k)] = (part_ref[k, core] + pair_ref[k]).astype(BF16).reshape(chips, per_device, channels)

    def sum_copy(i):
        peer = lax.rem(chip + i, chips)
        return remote(sum_ref.at[peer], got_ref.at[chip], g_send.at[i], g_recv.at[chip], 2 * peer + core)

    @pl.loop(1, chips)
    def _(i):
        sum_copy(i).start()
    own = pl.ds(pl.multiple_of(chip * per_device, per_device), per_device)
    for k in range(kernels):
        grad_ref[:, cols(k)] = part_ref[k, core, own, :] + pair_ref[k, own, :]

    @pl.loop(1, chips)
    def _(i):
        j = lax.rem(chip + i, chips)
        remote(sum_ref.at[j], got_ref.at[j], g_send.at[0], g_recv.at[j], pair).wait_recv()
        grad_ref[...] += got_ref[j].astype(F32)
        sum_copy(i).wait_send()

    @pl.loop(1, n)
    def _(i):
        j = peer_of(i)
        remote(band_ref.at[j], fg_ref.at[j], b_send.at[0], b_recv.at[j], pair).wait_recv()
        band_copy(i).wait_send()
        field_copy(i).wait_send()
    for k in range(kernels):
        pair_copy(k).wait_send()

    @pl.when(has_next)
    def _():
        for t in range(sections):
            up_copy(t).wait_send()
        for g in range(groups):
            row_copy(True, g).wait_send()

    @pl.when(has_prev)
    def _():
        for t in range(sections):
            down_copy(t).wait_send()
        for g in range(groups):
            row_copy(False, g).wait_send()


def local(fields, filter_basis, offsets, counts, mixing, cotangent):
    channels, columns = mixing.shape
    kernels = columns // channels
    _, taps, slots, block, outer = filter_basis.shape
    width = fields.shape[2]
    n = lax.axis_size("lon")
    per_device = channels // n
    groups = channels // 128
    sections = 3
    vmem = pl.BlockSpec(memory_space=pltpu.VMEM)
    smem = pl.BlockSpec(memory_space=pltpu.SMEM)

    live = jnp.arange(slots) < counts[0]
    basis = jnp.where(live[None, :, None, None], filter_basis[0], 0)
    w_adj = basis.transpose(0, 2, 1, 3).reshape(taps * block, slots * outer)
    w_fwd = basis.transpose(3, 1, 0, 2).reshape(outer, slots * taps * block)
    nblocks = width // block
    at = jnp.arange(nblocks, dtype=jnp.int32)[None, :]
    to = (at + offsets[0][:, None]) % nblocks
    source = (at - offsets[0][:, None]) % nblocks
    perm = spread_columns(channels, kernels, BF16)
    mix = lax.dot_general(mixing, perm, (((1,), (1,)), ((), ())), preferred_element_type=F32).astype(BF16)
    cot_t = cotangent[:, 0, :].T
    cot = cotangent.reshape(n // 2, 2, per_device, width).transpose(1, 0, 2, 3).reshape(channels, width)

    wide = (width, channels)
    dma = pltpu.SemaphoreType.DMA
    mixed_t, fg, grad = pl.pallas_call(
        functools.partial(fused_kernel, kernels, block, slots, sections),
        out_shape=[
            jax.ShapeDtypeStruct(wide, BF16),
            jax.ShapeDtypeStruct((n, per_device, width), BF16),
            jax.ShapeDtypeStruct((per_device, columns), F32),
        ],
        in_specs=[smem] * 2 + [vmem] * 6,
        out_specs=[vmem] * 3,
        scratch_shapes=[
            pltpu.VMEM((n, per_device, width), BF16),
            pltpu.VMEM((taps, width // block, block, channels), BF16),
            pltpu.VMEM((width // block, block, columns), BF16),
            pltpu.VMEM(wide, BF16),
            pltpu.VMEM(wide, F32),
            pltpu.VMEM(wide, BF16),
            pltpu.VMEM(wide, BF16),
            pltpu.VMEM(wide, BF16),
            pltpu.VMEM((n, per_device, width), BF16),
            pltpu.VMEM((kernels, 2, channels // 2, channels), F32),
            pltpu.VMEM((kernels, channels // 2, channels), F32),
            pltpu.VMEM((n // 2, per_device, columns), BF16),
            pltpu.VMEM((n // 2, per_device, columns), BF16),
            dma((n,)), dma((n,)),
            dma((2, groups)), dma((2, groups)),
            dma((2, sections)), dma((2, sections)),
            dma((n,)), dma((n,)),
            dma((kernels,)), dma((kernels,)),
            dma((n // 2,)), dma((n // 2,)),
        ],
        compiler_params=pltpu.CompilerParams(
            collective_id=0, has_side_effects=True, vmem_limit_bytes=56 * 2**20),
        cost_estimate=pl.CostEstimate(flops=6 * 10**10, bytes_accessed=10**7, transcendentals=0),
        name="fused",
    )(to, source, fields.transpose(1, 0, 2), cot_t, cot, mix, w_adj, w_fwd)
    grad = lax.dot(grad, spread_columns(channels, kernels, F32), precision=lax.Precision.HIGHEST)
    return mixed_t.T[:, None, :], fg.transpose(1, 0, 2), grad


def solution(mesh):
    in_specs = (
        P(("grp", "lon"), None, None),
        P("lon", None, None, None, None),
        P("lon", None),
        P("lon"),
        P(),
        P("grp", "lon", None),
    )
    out_specs = (P("grp", "lon", None), P(("grp", "lon"), None, None), P(("grp", "lon"), None))
    return jax.shard_map(local, mesh=mesh, in_specs=in_specs, out_specs=out_specs, check_vma=False)
```

```python
import functools

import jax
import jax.numpy as jnp
from jax import lax
from jax.experimental import pallas as pl
from jax.experimental.pallas import tpu as pltpu
from jax.sharding import PartitionSpec as P

F32 = jnp.float32
BF16 = jnp.bfloat16


def spread_columns(channels, kernels, dtype):
    size = channels * kernels
    row = lax.broadcasted_iota(jnp.int32, (size, size), 0)
    col = lax.broadcasted_iota(jnp.int32, (size, size), 1)
    return ((row % channels) * kernels + row // channels == col).astype(dtype)


def fused_kernel(kernels, block, slots, sections, to_ref, from_ref, live_ref, fields_ref, cot_t_ref, mixing_ref, basis_ref,
                 mixed_ref, fg_ref, grad_ref,
                 mix_ref, cot_ref, wa_ref, wf_ref, rows_ref, x_ref, gf_ref, a0_ref, a1_ref, a2_ref, h0_ref, h2_ref, band_ref,
                 part_ref, pair_ref, sum_ref, got_ref,
                 f_send, f_recv, x_send, x_recv, h_send, h_recv, b_send, b_recv, p_send, p_recv, g_send, g_recv):
    width, channels = cot_t_ref.shape
    nblocks = width // block
    n, per_device, _ = fields_ref.shape
    tile = 128
    groups = channels // tile
    per_group = tile // per_device
    me = lax.axis_index("lon")
    core = lax.rem(me, 2)
    pair = me + 1 - 2 * core
    cols = lambda k: slice(k * channels, (k + 1) * channels)
    has_prev, has_next = me > 0, me < n - 1

    def remote(src, dst, send, recv, device):
        return pltpu.make_async_remote_copy(
            src_ref=src, dst_ref=dst, send_sem=send, recv_sem=recv,
            device_id={"lon": device}, device_id_type=pl.DeviceIdType.MESH)

    def peer_of(i):
        return lax.rem(me + i, n)

    barrier = pltpu.get_barrier_semaphore()

    @pl.loop(1, n)
    def _(i):
        pl.semaphore_signal(barrier, inc=1, device_id={"lon": peer_of(i)}, device_id_type=pl.DeviceIdType.MESH)
    pl.semaphore_wait(barrier, n - 1)

    def field_copy(i):
        peer = peer_of(i)
        return remote(fields_ref.at[peer], rows_ref.at[me], f_send.at[i], f_recv.at[me], peer)

    @pl.loop(1, n)
    def _(i):
        field_copy(i).start()
    rows_ref[me] = fields_ref[me]

    @pl.when(jnp.logical_not(has_prev))
    def _():
        x_ref[0] = jnp.zeros((nblocks, block, channels), BF16)
        h2_ref[...] = jnp.zeros((width, channels), BF16)

    @pl.when(jnp.logical_not(has_next))
    def _():
        x_ref[2] = jnp.zeros((nblocks, block, channels), BF16)
        h0_ref[...] = jnp.zeros((width, channels), BF16)

    row = lax.broadcasted_iota(jnp.int32, (kernels * channels, channels), 0)
    col = lax.broadcasted_iota(jnp.int32, (kernels * channels, channels), 1)
    for k in range(kernels):
        pick = jnp.where(row == kernels * col + k, 1.0, 0.0).astype(BF16)
        mix_ref[:, cols(k)] = jnp.dot(mixing_ref[...], pick, preferred_element_type=F32).astype(BF16)
    taps = basis_ref.shape[0]
    outer = kernels * block
    for s in range(slots):
        for d in range(taps):
            piece = basis_ref[d, s].astype(F32) * live_ref[s]
            wa_ref[d * block:(d + 1) * block, s * outer:(s + 1) * outer] = piece.astype(BF16)
            at = (s * taps + d) * block
            wf_ref[:, at:at + block] = piece.T.astype(BF16)

    some = nblocks // 5
    rows = some * block

    @pl.loop(0, 5)
    def _(step):
        at = pl.ds(pl.multiple_of(step * rows, rows), rows)
        for k in range(kernels):
            gf_ref[pl.ds(step * some, some), :, cols(k)] = jnp.dot(
                cot_t_ref[at, :], mix_ref[:, cols(k)], preferred_element_type=F32
            ).astype(BF16).reshape(some, block, channels)

    piece = width // sections

    def down_copy(t):
        at = slice(t * piece, (t + 1) * piece)
        return remote(a0_ref.at[at], h0_ref.at[at], h_send.at[0, t], h_recv.at[0, t], me - 1)

    def up_copy(t):
        at = slice(t * piece, (t + 1) * piece)
        return remote(a2_ref.at[at], h2_ref.at[at], h_send.at[1, t], h_recv.at[1, t], me + 1)

    for t in range(sections):
        @pl.loop(t * (nblocks // sections), (t + 1) * (nblocks // sections))
        def _(b):
            parts = []
            for s in range(slots):
                found = gf_ref[from_ref[s, b]]
                for k in range(kernels):
                    parts.append(found[:, cols(k)])
            out = jnp.dot(wa_ref[...], jnp.concatenate(parts, axis=0), preferred_element_type=F32)
            at = pl.ds(pl.multiple_of(b * block, block), block)
            a0_ref[at, :] = out[:block].astype(BF16)
            a1_ref[at, :] = out[block:2 * block] + cot_t_ref[at, :].astype(F32)
            a2_ref[at, :] = out[2 * block:].astype(BF16)

        @pl.when(has_prev)
        def _():
            down_copy(t).start()

        @pl.when(has_next)
        def _():
            up_copy(t).start()

    for start in range(0, width, tile):
        stop = min(start + tile, width)
        cot_ref[:, start:stop] = cot_t_ref[start:stop, :].T

    def row_copy(to_next, g):
        at = (slice(None), slice(None), slice(g * tile, (g + 1) * tile))
        which, device = (0, me + 1) if to_next else (2, me - 1)
        return remote(x_ref.at[(1,) + at], x_ref.at[(which,) + at],
                      x_send.at[which // 2, g], x_recv.at[which // 2, g], device)

    for g in range(groups):
        @pl.loop(g * per_group, (g + 1) * per_group)
        def _(j):
            @pl.when(j != me)
            def _():
                remote(fields_ref.at[j], rows_ref.at[j], f_send.at[0], f_recv.at[j], pair).wait_recv()
        for start in range(0, width, tile):
            stop = min(start + tile, width)
            x_ref[1, start // block:stop // block, :, g * tile:(g + 1) * tile] = rows_ref[
                g * per_group:(g + 1) * per_group, :, start:stop
            ].reshape(tile, stop - start).T.reshape((stop - start) // block, block, tile)

        @pl.when(has_next)
        def _():
            row_copy(True, g).start()

        @pl.when(has_prev)
        def _():
            row_copy(False, g).start()

    for t in range(sections):
        @pl.when(has_next)
        def _():
            down_copy(t).wait_recv()

        @pl.when(has_prev)
        def _():
            up_copy(t).wait_recv()
    for start in range(0, width, tile):
        stop = min(start + tile, width)
        total = (a1_ref[start:stop] + h0_ref[start:stop].astype(F32) + h2_ref[start:stop].astype(F32)).astype(BF16)
        band_ref[:, :, start:stop] = total.T.reshape(n, per_device, stop - start)

    def band_copy(i):
        peer = peer_of(i)
        return remote(band_ref.at[peer], fg_ref.at[me], b_send.at[i], b_recv.at[me], peer)

    @pl.loop(1, n)
    def _(i):
        band_copy(i).start()
    fg_ref[me] = band_ref[me]

    for g in range(groups):
        @pl.when(has_prev)
        def _():
            row_copy(True, g).wait_recv()

        @pl.when(has_next)
        def _():
            row_copy(False, g).wait_recv()

    @pl.loop(0, nblocks)
    def _(b):
        parts = []
        for s in range(slots):
            for d in range(3):
                parts.append(x_ref[d, to_ref[s, b]])
        out = jnp.dot(wf_ref[...], jnp.concatenate(parts, axis=0), preferred_element_type=F32).astype(BF16)
        for k in range(kernels):
            gf_ref[b, :, cols(k)] = out[k * block:(k + 1) * block]

    chips = n // 2
    chip = me // 2

    def pair_copy(k):
        return remote(part_ref.at[k, :, 1 - core], pair_ref.at[k], p_send.at[k], p_recv.at[k], pair)

    for k in range(kernels):
        part_ref[k] = jnp.dot(
            cot_ref[...], gf_ref[:, :, cols(k)].reshape(width, channels), preferred_element_type=F32
        ).reshape(chips, 2, per_device, channels)
        pair_copy(k).start()

    @pl.loop(0, 5)
    def _(step):
        at = pl.ds(pl.multiple_of(step * rows, rows), rows)
        blocks = pl.ds(step * some, some)
        mixed = lax.dot_general(
            gf_ref[blocks].reshape(rows, kernels * channels), mix_ref[...],
            (((1,), (1,)), ((), ())), preferred_element_type=F32)
        mixed_ref[at, :] = (x_ref[1, blocks].reshape(rows, channels).astype(F32) + mixed).astype(BF16)

    for k in range(kernels):
        pair_copy(k).wait_recv()
        sum_ref[:, :, cols(k)] = (part_ref[k, :, core] + pair_ref[k]).astype(BF16)

    def sum_copy(i):
        peer = lax.rem(chip + i, chips)
        return remote(sum_ref.at[peer], got_ref.at[chip], g_send.at[i], g_recv.at[chip], 2 * peer + core)

    @pl.loop(1, chips)
    def _(i):
        sum_copy(i).start()
    for k in range(kernels):
        grad_ref[:, cols(k)] = part_ref[k, chip, core] + pair_ref[k, chip]

    @pl.loop(1, chips)
    def _(i):
        j = lax.rem(chip + i, chips)
        remote(sum_ref.at[j], got_ref.at[j], g_send.at[0], g_recv.at[j], pair).wait_recv()
        grad_ref[...] += got_ref[j].astype(F32)
        sum_copy(i).wait_send()

    @pl.loop(1, n)
    def _(i):
        j = peer_of(i)
        remote(band_ref.at[j], fg_ref.at[j], b_send.at[0], b_recv.at[j], pair).wait_recv()
        band_copy(i).wait_send()
        field_copy(i).wait_send()
    for k in range(kernels):
        pair_copy(k).wait_send()

    @pl.when(has_next)
    def _():
        for t in range(sections):
            up_copy(t).wait_send()
        for g in range(groups):
            row_copy(True, g).wait_send()

    @pl.when(has_prev)
    def _():
        for t in range(sections):
            down_copy(t).wait_send()
        for g in range(groups):
            row_copy(False, g).wait_send()


def local(fields, filter_basis, offsets, counts, mixing, cotangent):
    channels, columns = mixing.shape
    kernels = columns // channels
    _, taps, slots, block, outer = filter_basis.shape
    width = fields.shape[2]
    n = lax.axis_size("lon")
    per_device = channels // n
    groups = channels // 128
    sections = 3
    vmem = pl.BlockSpec(memory_space=pltpu.VMEM)
    smem = pl.BlockSpec(memory_space=pltpu.SMEM)

    live = (jnp.arange(slots) < counts[0]).astype(F32)
    nblocks = width // block
    at = jnp.arange(nblocks, dtype=jnp.int32)[None, :]
    to = (at + offsets[0][:, None]) % nblocks
    source = (at - offsets[0][:, None]) % nblocks
    cot_t = cotangent[:, 0, :].T

    wide = (width, channels)
    dma = pltpu.SemaphoreType.DMA
    mixed_t, fg, grad = pl.pallas_call(
        functools.partial(fused_kernel, kernels, block, slots, sections),
        out_shape=[
            jax.ShapeDtypeStruct(wide, BF16),
            jax.ShapeDtypeStruct((n, per_device, width), BF16),
            jax.ShapeDtypeStruct((per_device, columns), F32),
        ],
        in_specs=[smem] * 3 + [vmem] * 4,
        out_specs=[vmem] * 3,
        scratch_shapes=[
            pltpu.VMEM((channels, columns), BF16),
            pltpu.VMEM((channels, width), BF16),
            pltpu.VMEM((taps * block, slots * outer), BF16),
            pltpu.VMEM((outer, slots * taps * block), BF16),
            pltpu.VMEM((n, per_device, width), BF16),
            pltpu.VMEM((taps, width // block, block, channels), BF16),
            pltpu.VMEM((width // block, block, columns), BF16),
            pltpu.VMEM(wide, BF16),
            pltpu.VMEM(wide, F32),
            pltpu.VMEM(wide, BF16),
            pltpu.VMEM(wide, BF16),
            pltpu.VMEM(wide, BF16),
            pltpu.VMEM((n, per_device, width), BF16),
            pltpu.VMEM((kernels, n // 2, 2, per_device, channels), F32),
            pltpu.VMEM((kernels, n // 2, per_device, channels), F32),
            pltpu.VMEM((n // 2, per_device, columns), BF16),
            pltpu.VMEM((n // 2, per_device, columns), BF16),
            dma((n,)), dma((n,)),
            dma((2, groups)), dma((2, groups)),
            dma((2, sections)), dma((2, sections)),
            dma((n,)), dma((n,)),
            dma((kernels,)), dma((kernels,)),
            dma((n // 2,)), dma((n // 2,)),
        ],
        compiler_params=pltpu.CompilerParams(
            collective_id=0, has_side_effects=True, vmem_limit_bytes=58 * 2**20),
        cost_estimate=pl.CostEstimate(flops=6 * 10**10, bytes_accessed=10**7, transcendentals=0),
        name="fused",
    )(to, source, live, fields.transpose(1, 0, 2), cot_t, mixing, filter_basis[0])
    high = lax.reduce_precision(grad, exponent_bits=8, mantissa_bits=7)
    grad = jnp.dot(
        jnp.concatenate([high, grad - high]).astype(BF16), spread_columns(channels, kernels, BF16), preferred_element_type=F32)
    grad = grad[:per_device] + grad[per_device:]
    return mixed_t.T[:, None, :], fg.transpose(1, 0, 2), grad


def solution(mesh):
    in_specs = (
        P(("grp", "lon"), None, None),
        P("lon", None, None, None, None),
        P("lon", None),
        P("lon"),
        P(),
        P("grp", "lon", None),
    )
    out_specs = (P("grp", "lon", None), P(("grp", "lon"), None, None), P(("grp", "lon"), None))
    return jax.shard_map(local, mesh=mesh, in_specs=in_specs, out_specs=out_specs, check_vma=False)
```

```python
import functools

import jax
import jax.numpy as jnp
from jax import lax
from jax.experimental import pallas as pl
from jax.experimental.pallas import tpu as pltpu
from jax.sharding import PartitionSpec as P

F32 = jnp.float32
BF16 = jnp.bfloat16


def spread_columns(channels, kernels, dtype):
    size = channels * kernels
    row = lax.broadcasted_iota(jnp.int32, (size, size), 0)
    col = lax.broadcasted_iota(jnp.int32, (size, size), 1)
    return ((row % channels) * kernels + row // channels == col).astype(dtype)


def fused_kernel(kernels, block, slots, sections, to_ref, from_ref, live_ref, fields_ref, cot_t_ref, mixing_ref, basis_ref,
                 mixed_ref, fg_ref, grad_ref,
                 mix_ref, cot_ref, wa_ref, wf_ref, rows_ref, x_ref, gf_ref, a0_ref, a1_ref, a2_ref, h0_ref, h2_ref, band_ref,
                 part_ref, pair_ref, sum_ref, got_ref,
                 f_send, f_recv, x_send, x_recv, h_send, h_recv, b_send, b_recv, p_send, p_recv, g_send, g_recv):
    width, channels = cot_t_ref.shape
    nblocks = width // block
    n, per_device, _ = fields_ref.shape
    tile = 128
    groups = channels // tile
    per_group = tile // per_device
    me = lax.axis_index("lon")
    core = lax.rem(me, 2)
    pair = me + 1 - 2 * core
    cols = lambda k: slice(k * channels, (k + 1) * channels)
    has_prev, has_next = me > 0, me < n - 1

    def remote(src, dst, send, recv, device):
        return pltpu.make_async_remote_copy(
            src_ref=src, dst_ref=dst, send_sem=send, recv_sem=recv,
            device_id={"lon": device}, device_id_type=pl.DeviceIdType.MESH)

    def peer_of(i):
        return lax.rem(me + i, n)

    barrier = pltpu.get_barrier_semaphore()

    @pl.loop(1, n)
    def _(i):
        pl.semaphore_signal(barrier, inc=1, device_id={"lon": peer_of(i)}, device_id_type=pl.DeviceIdType.MESH)
    pl.semaphore_wait(barrier, n - 1)

    def field_copy(i):
        peer = peer_of(i)
        return remote(fields_ref.at[peer], rows_ref.at[me], f_send.at[i], f_recv.at[me], peer)

    @pl.loop(1, n)
    def _(i):
        field_copy(i).start()
    rows_ref[me] = fields_ref[me]

    @pl.when(jnp.logical_not(has_prev))
    def _():
        x_ref[0] = jnp.zeros((nblocks, block, channels), BF16)
        h2_ref[...] = jnp.zeros((width, channels), BF16)

    @pl.when(jnp.logical_not(has_next))
    def _():
        x_ref[2] = jnp.zeros((nblocks, block, channels), BF16)
        h0_ref[...] = jnp.zeros((width, channels), BF16)

    row = lax.broadcasted_iota(jnp.int32, (kernels * channels, channels), 0)
    col = lax.broadcasted_iota(jnp.int32, (kernels * channels, channels), 1)
    for k in range(kernels):
        pick = jnp.where(row == kernels * col + k, 1.0, 0.0).astype(BF16)
        mix_ref[:, cols(k)] = jnp.dot(mixing_ref[...], pick, preferred_element_type=F32).astype(BF16)
    taps = basis_ref.shape[0]
    outer = kernels * block
    for s in range(slots):
        for d in range(taps):
            piece = basis_ref[d, s].astype(F32) * live_ref[s]
            wa_ref[d * block:(d + 1) * block, s * outer:(s + 1) * outer] = piece.astype(BF16)
            at = (s * taps + d) * block
            wf_ref[:, at:at + block] = piece.T.astype(BF16)

    some = nblocks // 5
    rows = some * block

    @pl.loop(0, 5)
    def _(step):
        at = pl.ds(pl.multiple_of(step * rows, rows), rows)
        for k in range(kernels):
            gf_ref[pl.ds(step * some, some), :, cols(k)] = jnp.dot(
                cot_t_ref[at, :], mix_ref[:, cols(k)], preferred_element_type=F32
            ).astype(BF16).reshape(some, block, channels)

    piece = width // sections

    def down_copy(t):
        at = slice(t * piece, (t + 1) * piece)
        return remote(a0_ref.at[at], h0_ref.at[at], h_send.at[0, t], h_recv.at[0, t], me - 1)

    def up_copy(t):
        at = slice(t * piece, (t + 1) * piece)
        return remote(a2_ref.at[at], h2_ref.at[at], h_send.at[1, t], h_recv.at[1, t], me + 1)

    for t in range(sections):
        @pl.loop(t * (nblocks // sections), (t + 1) * (nblocks // sections))
        def _(b):
            parts = []
            for s in range(slots):
                found = gf_ref[from_ref[s, b]]
                for k in range(kernels):
                    parts.append(found[:, cols(k)])
            out = jnp.dot(wa_ref[...], jnp.concatenate(parts, axis=0), preferred_element_type=F32)
            at = pl.ds(pl.multiple_of(b * block, block), block)
            a0_ref[at, :] = out[:block].astype(BF16)
            a1_ref[at, :] = out[block:2 * block] + cot_t_ref[at, :].astype(F32)
            a2_ref[at, :] = out[2 * block:].astype(BF16)

        @pl.when(has_prev)
        def _():
            down_copy(t).start()

        @pl.when(has_next)
        def _():
            up_copy(t).start()

    for start in range(0, width, tile):
        stop = min(start + tile, width)
        cot_ref[:, start:stop] = cot_t_ref[start:stop, :].T

    def lanes(g):
        return pl.ds(g * tile if isinstance(g, int) else pl.multiple_of(g * tile, tile), tile)

    def row_copy(to_next, g):
        at = (slice(None), slice(None), lanes(g))
        which, device = (0, me + 1) if to_next else (2, me - 1)
        return remote(x_ref.at[(1,) + at], x_ref.at[(which,) + at],
                      x_send.at[which // 2, g], x_recv.at[which // 2, g], device)

    for turn in range(groups):
        g = lax.rem(me // per_group + turn, groups)

        @pl.loop(0, per_group)
        def _(i):
            j = g * per_group + i

            @pl.when(j != me)
            def _():
                remote(fields_ref.at[j], rows_ref.at[j], f_send.at[0], f_recv.at[j], pair).wait_recv()
        for start in range(0, width, tile):
            stop = min(start + tile, width)
            x_ref[1, start // block:stop // block, :, lanes(g)] = rows_ref[
                pl.ds(g * per_group, per_group), :, start:stop
            ].reshape(tile, stop - start).T.reshape((stop - start) // block, block, tile)

        @pl.when(has_next)
        def _():
            row_copy(True, g).start()

        @pl.when(has_prev)
        def _():
            row_copy(False, g).start()

    for t in range(sections):
        @pl.when(has_next)
        def _():
            down_copy(t).wait_recv()

        @pl.when(has_prev)
        def _():
            up_copy(t).wait_recv()
    for start in range(0, width, tile):
        stop = min(start + tile, width)
        total = (a1_ref[start:stop] + h0_ref[start:stop].astype(F32) + h2_ref[start:stop].astype(F32)).astype(BF16)
        band_ref[:, :, start:stop] = total.T.reshape(n, per_device, stop - start)

    def band_copy(i):
        peer = peer_of(i)
        return remote(band_ref.at[peer], fg_ref.at[me], b_send.at[i], b_recv.at[me], peer)

    @pl.loop(1, n)
    def _(i):
        band_copy(i).start()
    fg_ref[me] = band_ref[me]

    for g in range(groups):
        @pl.when(has_prev)
        def _():
            row_copy(True, g).wait_recv()

        @pl.when(has_next)
        def _():
            row_copy(False, g).wait_recv()

    @pl.loop(0, nblocks)
    def _(b):
        parts = []
        for s in range(slots):
            for d in range(3):
                parts.append(x_ref[d, to_ref[s, b]])
        out = jnp.dot(wf_ref[...], jnp.concatenate(parts, axis=0), preferred_element_type=F32).astype(BF16)
        for k in range(kernels):
            gf_ref[b, :, cols(k)] = out[k * block:(k + 1) * block]

    chips = n // 2
    chip = me // 2

    def pair_copy(k):
        return remote(part_ref.at[k, :, 1 - core], pair_ref.at[k], p_send.at[k], p_recv.at[k], pair)

    for k in range(kernels):
        part_ref[k] = jnp.dot(
            cot_ref[...], gf_ref[:, :, cols(k)].reshape(width, channels), preferred_element_type=F32
        ).reshape(chips, 2, per_device, channels)
        pair_copy(k).start()

    @pl.loop(0, 5)
    def _(step):
        at = pl.ds(pl.multiple_of(step * rows, rows), rows)
        blocks = pl.ds(step * some, some)
        mixed = lax.dot_general(
            gf_ref[blocks].reshape(rows, kernels * channels), mix_ref[...],
            (((1,), (1,)), ((), ())), preferred_element_type=F32)
        mixed_ref[at, :] = (x_ref[1, blocks].reshape(rows, channels).astype(F32) + mixed).astype(BF16)

    for k in range(kernels):
        pair_copy(k).wait_recv()
        sum_ref[:, :, cols(k)] = (part_ref[k, :, core] + pair_ref[k]).astype(BF16)

    def sum_copy(i):
        peer = lax.rem(chip + i, chips)
        return remote(sum_ref.at[peer], got_ref.at[chip], g_send.at[i], g_recv.at[chip], 2 * peer + core)

    @pl.loop(1, chips)
    def _(i):
        sum_copy(i).start()
    for k in range(kernels):
        grad_ref[:, cols(k)] = part_ref[k, chip, core] + pair_ref[k, chip]

    @pl.loop(1, chips)
    def _(i):
        j = lax.rem(chip + i, chips)
        remote(sum_ref.at[j], got_ref.at[j], g_send.at[0], g_recv.at[j], pair).wait_recv()
        grad_ref[...] += got_ref[j].astype(F32)
        sum_copy(i).wait_send()

    @pl.loop(1, n)
    def _(i):
        j = peer_of(i)
        remote(band_ref.at[j], fg_ref.at[j], b_send.at[0], b_recv.at[j], pair).wait_recv()
        band_copy(i).wait_send()
        field_copy(i).wait_send()
    for k in range(kernels):
        pair_copy(k).wait_send()

    @pl.when(has_next)
    def _():
        for t in range(sections):
            up_copy(t).wait_send()
        for g in range(groups):
            row_copy(True, g).wait_send()

    @pl.when(has_prev)
    def _():
        for t in range(sections):
            down_copy(t).wait_send()
        for g in range(groups):
            row_copy(False, g).wait_send()


def local(fields, filter_basis, offsets, counts, mixing, cotangent):
    channels, columns = mixing.shape
    kernels = columns // channels
    _, taps, slots, block, outer = filter_basis.shape
    width = fields.shape[2]
    n = lax.axis_size("lon")
    per_device = channels // n
    groups = channels // 128
    sections = 3
    vmem = pl.BlockSpec(memory_space=pltpu.VMEM)
    smem = pl.BlockSpec(memory_space=pltpu.SMEM)

    live = (jnp.arange(slots) < counts[0]).astype(F32)
    nblocks = width // block
    at = jnp.arange(nblocks, dtype=jnp.int32)[None, :]
    to = (at + offsets[0][:, None]) % nblocks
    source = (at - offsets[0][:, None]) % nblocks
    cot_t = cotangent[:, 0, :].T

    wide = (width, channels)
    dma = pltpu.SemaphoreType.DMA
    mixed_t, fg, grad = pl.pallas_call(
        functools.partial(fused_kernel, kernels, block, slots, sections),
        out_shape=[
            jax.ShapeDtypeStruct(wide, BF16),
            jax.ShapeDtypeStruct((n, per_device, width), BF16),
            jax.ShapeDtypeStruct((per_device, columns), F32),
        ],
        in_specs=[smem] * 3 + [vmem] * 4,
        out_specs=[vmem] * 3,
        scratch_shapes=[
            pltpu.VMEM((channels, columns), BF16),
            pltpu.VMEM((channels, width), BF16),
            pltpu.VMEM((taps * block, slots * outer), BF16),
            pltpu.VMEM((outer, slots * taps * block), BF16),
            pltpu.VMEM((n, per_device, width), BF16),
            pltpu.VMEM((taps, width // block, block, channels), BF16),
            pltpu.VMEM((width // block, block, columns), BF16),
            pltpu.VMEM(wide, BF16),
            pltpu.VMEM(wide, F32),
            pltpu.VMEM(wide, BF16),
            pltpu.VMEM(wide, BF16),
            pltpu.VMEM(wide, BF16),
            pltpu.VMEM((n, per_device, width), BF16),
            pltpu.VMEM((kernels, n // 2, 2, per_device, channels), F32),
            pltpu.VMEM((kernels, n // 2, per_device, channels), F32),
            pltpu.VMEM((n // 2, per_device, columns), BF16),
            pltpu.VMEM((n // 2, per_device, columns), BF16),
            dma((n,)), dma((n,)),
            dma((2, groups)), dma((2, groups)),
            dma((2, sections)), dma((2, sections)),
            dma((n,)), dma((n,)),
            dma((kernels,)), dma((kernels,)),
            dma((n // 2,)), dma((n // 2,)),
        ],
        compiler_params=pltpu.CompilerParams(
            collective_id=0, has_side_effects=True, vmem_limit_bytes=58 * 2**20),
        cost_estimate=pl.CostEstimate(flops=6 * 10**10, bytes_accessed=10**7, transcendentals=0),
        name="fused",
    )(to, source, live, fields.transpose(1, 0, 2), cot_t, mixing, filter_basis[0])
    high = lax.reduce_precision(grad, exponent_bits=8, mantissa_bits=7)
    grad = jnp.dot(
        jnp.concatenate([high, grad - high]).astype(BF16), spread_columns(channels, kernels, BF16), preferred_element_type=F32)
    grad = grad[:per_device] + grad[per_device:]
    return mixed_t.T[:, None, :], fg.transpose(1, 0, 2), grad


def solution(mesh):
    in_specs = (
        P(("grp", "lon"), None, None),
        P("lon", None, None, None, None),
        P("lon", None),
        P("lon"),
        P(),
        P("grp", "lon", None),
    )
    out_specs = (P("grp", "lon", None), P(("grp", "lon"), None, None), P(("grp", "lon"), None))
    return jax.shard_map(local, mesh=mesh, in_specs=in_specs, out_specs=out_specs, check_vma=False)
```
